32 devices in a mesh: groups: 2 (over x), seq: 8 (over z, y), head: 2 (over core).
Axes of the slice: x: 2, y: 2, z: 4, core: 2. Of those that a mesh axis runs over, the one named last changes fastest.
Arguments:
- queries: bfloat16 [4096, 2048], P(('groups', 'seq'), 'head'), parts along dimension 0, may hold values from -24 to 24
- key_vectors: bfloat16 [4096, 2048], P(('groups', 'seq'), 'head'), parts along dimension 0, may hold values from -9 to 9
- value_vectors: bfloat16 [4096, 2048], P(('groups', 'seq'), 'head'), parts along dimension 0, may hold values from -6 to 6
- frozen_grad: bfloat16 [4096, 2048], P(('groups', 'seq'), 'head'), parts along dimension 0, may hold values from -6 to 6
- output_grad: bfloat16 [4096, 5376], P(('groups', 'seq'), 'head'), parts along dimension 0, may hold values from -6 to 6
- document_ids: int32 [4096], P('groups'), parts along dimension 0, may hold values from 0 to 7, never falling along the last dimension, each value on 1 to 768 neighbouring positions
- document_tenant: int32 [16], P('groups'), parts along dimension 0, may hold values from 0 to 7
- tenant_owner: int32 [8], replicated, may hold values from 0 to 7, each once
- phm_rule: float32 [16, 4, 4, 4], P('groups'), parts along dimension 0, may hold values from -3 to 3
- phm_left: float32 [16, 4, 512], P('groups'), parts along dimension 0, may hold values from -3 to 3
- phm_right: float32 [16, 4, 1344], P('groups'), parts along dimension 0, may hold values from -0.15625 to 0.15625
Outputs:
- query_grad: bfloat16 [4096, 2048], P(('groups', 'seq'), 'head'), parts along dimension 0
- key_grad: bfloat16 [4096, 2048], P(('groups', 'seq'), 'head'), parts along dimension 0
- value_grad: bfloat16 [4096, 2048], P(('groups', 'seq'), 'head'), parts along dimension 0
- rule_grad: float32 [16, 4, 4, 4], P(('groups', 'seq'), 'head'), parts along dimension 0
- left_grad: float32 [16, 4, 512], P(('groups', 'seq'), 'head'), parts along dimension 0
- right_grad: float32 [16, 4, 1344], P(('groups', 'seq'), 'head'), parts along dimension 0
The draws below stay inside these ranges and needn't reach their ends.
There are 2 independent parts, one for each index of `groups`. The reference program is written for one: setup_inputs(seed, part) draws one part's arguments, and reference() takes and returns one part's arrays. A program takes and returns all parts, laid end to end along the dimension named above; an argument that names none is the same for every part. Nothing has to cross between parts.
Inputs may be any that keep to these rules, and one draw needn't show every extreme that they name: `document_ids`: never falling; each document holds 1 to 768 tokens, one exactly 768. `tenant_owner`: each seq index owns exactly one tenant.
All inputs are finite; a program needn't handle non-finite values.
Results may differ from the reference program's by a relative error of at most 0.009.
Values may be sent and summed in bfloat16 or wider, within the bound.
A program may use at most 128 MiB of HBM per device.

```python
import math
import jax
import jax.numpy as jnp
import numpy as np
from jax import lax

D = 5376
HEADS = 16
HEAD_DIM = 128
WINDOW = 512
PHM_N = 4
TOK_DEV = 256
REACH = 2
TOKENS = 2048
DOCS = 8
DOC_MOST = 768
TENANTS = 8
SUB_LEFT = 512
SUB_RIGHT = 1344


def drawn_pair(key):
    width = HEADS * HEAD_DIM
    base_query = jnp.clip(jax.random.normal(jax.random.fold_in(key, 101), (TOKENS, width), jnp.float32), -4.0, 4.0)
    base_key = jnp.clip(jax.random.normal(jax.random.fold_in(key, 102), (TOKENS, width), jnp.float32), -4.0, 4.0)
    query_side = base_query
    key_side = base_key
    return (query_side, key_side)


def draw_queries(key, part):
    return drawn_pair(key)[0].astype(jnp.bfloat16)


def draw_key_vectors(key, part):
    return drawn_pair(key)[1].astype(jnp.bfloat16)


def set_ends(array, own_key, low, high):
    extent = array.shape
    spot = [jax.random.randint(jax.random.fold_in(own_key, axis), (), 0, extent[axis]) for axis in range(len(extent))]
    array = array.at[tuple(spot)].set(low)
    longest = extent.index(max(extent))
    spot[longest] = (spot[longest] + 1) % extent[longest]
    return array.at[tuple(spot)].set(high)


def steps_of(stream_key, extent, shards, low, largest):
    factor_of = 1.0
    for position, blocks in shards:
        draws = jax.random.uniform(jax.random.fold_in(jax.random.fold_in(stream_key, 6), position), (blocks,), jnp.float32, low / len(shards), largest / len(shards))
        factor_of = factor_of * jnp.repeat(jnp.exp(draws), extent[position] // blocks).reshape((-1,) + (1,) * (len(extent) - 1 - position))
    return factor_of


def rank_table(amount, slope):
    loads = [(1 << 20) // math.isqrt(rank ** slope) + 1 for rank in range(1, amount + 1)]
    spread = 1 + sum(loads) // (1 << 30)
    return np.cumsum(np.array([max(1, weight // spread) for weight in loads]))


def ranked_ids(key, shape, number_of, slope):
    listing = rank_table(number_of, slope)
    ticket = jax.random.randint(jax.random.fold_in(key, 1), shape, 0, int(listing[number_of - 1]))
    grade = jnp.searchsorted(jnp.asarray(listing, jnp.int32), ticket, side="right")
    return jax.random.permutation(jax.random.fold_in(key, 2), number_of)[grade].astype(jnp.int32)


def length_profile(number_of, total, limit, lean):
    portions = [(1 << 20) // math.isqrt(rank ** lean) + 1 for rank in range(2, number_of + 1)]
    spare, given = total - limit - (number_of - 1), [1] * (number_of - 1)
    while spare > 0:
        candidates = [i for i in range(number_of - 1) if given[i] < limit]
        pool, budget = sum([portions[i] for i in candidates]), spare
        for i in candidates:
            addition = min(limit - given[i], max(1, budget * portions[i] // pool), spare)
            given[i] = given[i] + addition
            spare = spare - addition
    return np.array([limit] + given)


def uneven(key, number_of, total, most, slope):
    if number_of == 2:
        one = jax.random.randint(key, (), max(1, total - most), min(most, total - 1) + 1)
        return jnp.stack([one, total - one])
    lengths = jnp.asarray(length_profile(number_of, total, most, slope), jnp.int32)
    pairs = (number_of - 1) // 2
    donor, sink = lengths[1:1 + 2 * pairs:2], lengths[2:2 + 2 * pairs:2]
    room = jnp.minimum(donor - 1, most - sink)
    moved = jax.random.randint(jax.random.fold_in(key, 1), (pairs,), 0, 1 << 20) % (room + 1)
    lengths = lengths.at[1:1 + 2 * pairs:2].set(donor - moved).at[2:2 + 2 * pairs:2].set(sink + moved)
    return lengths[jax.random.permutation(jax.random.fold_in(key, 2), number_of)]


def noise(stream_key, dims, scale, bound, shards=(), kind=jnp.bfloat16):
    result = jax.random.normal(stream_key, dims, jnp.float32) * scale
    if len(shards) > 0:
        result = steps_of(stream_key, dims, shards, -0.22, 0.18) * result
    return jnp.clip(result, min=-bound, max=bound).astype(kind)


def setup_inputs(seed: int = 0, part: int = 0) -> dict:
    splits = jax.random.split(jax.random.key(seed), 12)
    own_keys = jax.random.split(jax.random.fold_in(splits[11], part), 12)
    queries = draw_queries(jax.random.fold_in(jax.random.fold_in(splits[11], part), 71), part)
    key_vectors = draw_key_vectors(jax.random.fold_in(jax.random.fold_in(splits[11], part), 71), part)
    value_vectors = noise(own_keys[2], (TOKENS, HEADS * HEAD_DIM), 1.0, 6.0, ((0, 8), (1, 2)))
    frozen_grad = noise(own_keys[3], (TOKENS, HEADS * HEAD_DIM), 1.0, 6.0, ((0, 8), (1, 2)))
    output_grad = noise(own_keys[4], (TOKENS, D), 1.0, 6.0, ((0, 8), (1, 2)))
    document_ids = jnp.searchsorted(jnp.cumsum(uneven(own_keys[5], DOCS, TOKENS, DOC_MOST, 2)), jnp.arange(TOKENS), side="right").astype(jnp.int32)
    document_tenant = set_ends(ranked_ids(own_keys[6], (DOCS,), TENANTS, 2), jax.random.fold_in(own_keys[6], 3), 0, TENANTS - 1).astype(jnp.int32)
    tenant_owner = jax.random.permutation(splits[7], TENANTS).astype(jnp.int32)
    phm_rule = noise(own_keys[8], (TENANTS, PHM_N, PHM_N, PHM_N), 0.5, 3.0, (), jnp.float32)
    phm_left = noise(own_keys[9], (TENANTS, PHM_N, SUB_LEFT), 0.5, 3.0, (), jnp.float32)
    phm_right = noise(own_keys[10], (TENANTS, PHM_N, SUB_RIGHT), SUB_RIGHT ** -0.5, 0.15625, (), jnp.float32)
    return dict(queries=queries, key_vectors=key_vectors, value_vectors=value_vectors, frozen_grad=frozen_grad, output_grad=output_grad, document_ids=document_ids, document_tenant=document_tenant, tenant_owner=tenant_owner, phm_rule=phm_rule, phm_left=phm_left, phm_right=phm_right)


score_scale = 168.0 ** -0.5
neg_big = -1e30
highest = lax.Precision.HIGHEST


def band_mask(query_pos, key_pos, query_docs, key_docs):
    later = query_pos[:, None] - key_pos[None, :]
    inside = (key_pos[None, :] >= 0) & (later >= 0) & (later < WINDOW)
    return inside & (query_docs[:, None] == key_docs[None, :])


def attend(query_part, key_part, value_part, cot_part, allowed):
    query_wide = query_part.astype(jnp.float32)
    key_wide = key_part.astype(jnp.float32)
    value_wide = value_part.astype(jnp.float32)
    cot_wide = cot_part.astype(jnp.float32)
    scores = jnp.einsum("qgd,kgd->gqk", query_wide, key_wide) * score_scale
    scores = jnp.where(allowed[None], scores, neg_big)
    row_max = jnp.max(scores, axis=2, keepdims=True)
    expo_terms = jnp.exp(scores - row_max)
    attn_prob = expo_terms / jnp.sum(expo_terms, axis=2, keepdims=True)
    prob_low = attn_prob.astype(jnp.bfloat16).astype(jnp.float32)
    attn_out = jnp.einsum("gqk,kgd->qgd", prob_low, value_wide).astype(jnp.bfloat16)
    prob_grad = jnp.einsum("qgd,kgd->gqk", cot_wide, value_wide)
    row_dot = jnp.sum(attn_prob * prob_grad, axis=2, keepdims=True)
    dscore = (attn_prob * (prob_grad - row_dot)).astype(jnp.bfloat16).astype(jnp.float32)
    query_term = jnp.einsum("gqk,kgd->qgd", dscore, key_wide) * score_scale
    key_term = jnp.einsum("gqk,qgd->kgd", dscore, query_wide) * score_scale
    value_term = jnp.einsum("gqk,qgd->kgd", prob_low, cot_wide)
    return attn_out, query_term, key_term, value_term


def by_owner(grads, tenant_owner):
    return jnp.zeros_like(grads).at[tenant_owner].set(grads)


def reference(queries, key_vectors, value_vectors, frozen_grad, output_grad, document_ids, document_tenant, tenant_owner, phm_rule, phm_left, phm_right):
    seq_rows = queries.shape[0]
    block_total = seq_rows // TOK_DEV
    lead_rows = REACH * TOK_DEV
    key_span = (REACH + 1) * TOK_DEV
    head_shape = (seq_rows, HEADS, HEAD_DIM)
    tenant = document_tenant[document_ids]
    token_hot = (tenant[:, None] == jnp.arange(TENANTS, dtype=jnp.int32)[None, :]).astype(jnp.float32)
    cotangent = output_grad.astype(jnp.float32).reshape(seq_rows, PHM_N, SUB_RIGHT)
    gate_terms = jnp.einsum("tbq,tiq->tib", cotangent, phm_right[tenant], precision=highest)
    rule_tok = phm_rule[tenant]
    rule_mix = jnp.einsum("tiab,tib->tia", rule_tok, gate_terms, precision=highest)
    left_tok = phm_left[tenant]
    adapter = jnp.einsum("tia,tip->tap", rule_mix, left_tok, precision=highest)
    out_cot = (frozen_grad.astype(jnp.float32) + adapter.reshape(seq_rows, -1)).astype(jnp.bfloat16).reshape(head_shape)
    query_heads = queries.reshape(head_shape)
    lead_zero = jnp.zeros((lead_rows, HEADS, HEAD_DIM), jnp.bfloat16)
    key_lead = jnp.concatenate([lead_zero, key_vectors.reshape(head_shape)], axis=0)
    value_lead = jnp.concatenate([lead_zero, value_vectors.reshape(head_shape)], axis=0)
    doc_lead = jnp.concatenate([jnp.zeros((lead_rows,), jnp.int32), document_ids.astype(jnp.int32)])

    def block_step(totals, block_index):
        row_start = (block_index * TOK_DEV).astype(jnp.int32)
        query_pos = row_start + jnp.arange(TOK_DEV, dtype=jnp.int32)
        key_pos = row_start - lead_rows + jnp.arange(key_span, dtype=jnp.int32)
        query_docs = lax.dynamic_slice_in_dim(document_ids.astype(jnp.int32), row_start, TOK_DEV)
        key_docs = lax.dynamic_slice_in_dim(doc_lead, row_start, key_span)
        allowed = band_mask(query_pos, key_pos, query_docs, key_docs)
        attn_out, query_term, key_term, value_term = attend(
            lax.dynamic_slice_in_dim(query_heads, row_start, TOK_DEV, 0),
            lax.dynamic_slice_in_dim(key_lead, row_start, key_span, 0),
            lax.dynamic_slice_in_dim(value_lead, row_start, key_span, 0),
            lax.dynamic_slice_in_dim(out_cot, row_start, TOK_DEV, 0),
            allowed)
        key_acc, value_acc = totals
        key_acc = lax.dynamic_update_slice_in_dim(key_acc, lax.dynamic_slice_in_dim(key_acc, row_start, key_span, 0) + key_term, row_start, 0)
        value_acc = lax.dynamic_update_slice_in_dim(value_acc, lax.dynamic_slice_in_dim(value_acc, row_start, key_span, 0) + value_term, row_start, 0)
        return (key_acc, value_acc), (attn_out, query_term)

    zero_acc = jnp.zeros((lead_rows + seq_rows, HEADS, HEAD_DIM), jnp.float32)
    (key_acc, value_acc), (attn_blocks, query_blocks) = lax.scan(block_step, (zero_acc, zero_acc), jnp.arange(block_total, dtype=jnp.int32))
    query_grad = query_blocks.reshape(seq_rows, -1).astype(jnp.bfloat16)
    key_grad = key_acc[lead_rows:].reshape(seq_rows, -1).astype(jnp.bfloat16)
    value_grad = value_acc[lead_rows:].reshape(seq_rows, -1).astype(jnp.bfloat16)
    left_in = attn_blocks.reshape(seq_rows, PHM_N, SUB_LEFT).astype(jnp.float32)
    left_proj = jnp.einsum("tap,tip->tia", left_in, left_tok, precision=highest)
    rule_proj = jnp.einsum("tia,tiab->tib", left_proj, rule_tok, precision=highest)
    grad_scale = TOK_DEV ** -0.5
    rule_sum = grad_scale * jnp.einsum("tx,tia,tib->xiab", token_hot, left_proj, gate_terms, precision=highest)
    left_sum = grad_scale * jnp.einsum("tx,tia,tap->xip", token_hot, rule_mix, left_in, precision=highest)
    right_sum = grad_scale * jnp.einsum("tx,tib,tbq->xiq", token_hot, rule_proj, cotangent, precision=highest)
    return (query_grad, key_grad, value_grad,
            by_owner(rule_sum, tenant_owner), by_owner(left_sum, tenant_owner), by_owner(right_sum, tenant_owner))
```

```python
import functools

import jax
import jax.numpy as jnp
from jax import lax
from jax.experimental import pallas as pl
from jax.experimental.pallas import tpu as pltpu
from jax.sharding import PartitionSpec as P

HEAD_DIM = 128
WINDOW = 512
PHM_N = 4
MESH = pl.DeviceIdType.MESH

score_scale = 168.0 ** (-0.5)
neg_big = -1e30
f32 = jnp.float32
bf16 = jnp.bfloat16


def passed_along(value, axis, steps):
    count = lax.axis_size(axis)
    first, last = (max(0, -steps), min(count, count - steps))
    return lax.ppermute(value, axis, [(source, source + steps) for source in range(first, last)])


def split_two(value):
    high = lax.reduce_precision(value, 8, 7)
    return high.astype(bf16), (value - high).astype(bf16)


def kernel_split(value):
    high = value.astype(bf16)
    return high, (value - high.astype(f32)).astype(bf16)


def dot_nt(a, b):
    return lax.dot_general(a, b, (((1,), (1,)), ((), ())), preferred_element_type=f32)


def dot_nn(a, b):
    return lax.dot_general(a, b, (((1,), (0,)), ((), ())), preferred_element_type=f32)


def dot_tn(a, b):
    return lax.dot_general(a, b, (((0,), (0,)), ((), ())), preferred_element_type=f32)


def attention_kernel(reach, heads_per_block, *refs):
    blocks = reach + 1
    q_ref, frozen_ref = refs[0:2]
    k_refs = refs[2 : 2 + blocks]
    v_refs = refs[2 + blocks : 2 + 2 * blocks]
    gate_ref, qinfo_ref, kdoc_ref, rule_ref, lhi_ref, llo_ref = refs[2 + 2 * blocks : 8 + 2 * blocks]
    dq_ref, own_ref = refs[8 + 2 * blocks : 10 + 2 * blocks]
    back_refs = refs[10 + 2 * blocks : 10 + 2 * blocks + reach]
    proj_ref, left_ref, bias_ref = refs[10 + 2 * blocks + reach :]
    rows = q_ref.shape[0]
    head = pl.program_id(0)
    block = head // heads_per_block
    part = lax.rem(head, heads_per_block)

    @pl.when(head == 0)
    def _():
        query_pos = lax.broadcasted_iota(jnp.int32, (rows, rows), 0)
        key_pos = lax.broadcasted_iota(jnp.int32, (rows, rows), 1)
        for j in range(blocks):
            later = query_pos - key_pos + (reach - j) * rows
            same = qinfo_ref[:, 0:1] == kdoc_ref[:, j * rows : (j + 1) * rows]
            allowed = same & (later >= 0) & (later < WINDOW)
            bias_ref[:, j * rows : (j + 1) * rows] = jnp.where(allowed, 0.0, neg_big)

    mix = jnp.zeros(gate_ref.shape[1:], f32)
    for b in range(PHM_N):
        mix = mix + gate_ref[b] * rule_ref[block, b : b + 1, :]
    mix_hi, mix_lo = kernel_split(mix)
    columns = pl.ds(pl.multiple_of(part * HEAD_DIM, HEAD_DIM), HEAD_DIM)
    lhi = lhi_ref[:, columns]
    llo = llo_ref[:, columns]
    adapter = dot_nn(mix_hi, lhi) + dot_nn(mix_lo, lhi) + dot_nn(mix_hi, llo)
    cot = (frozen_ref[...].astype(f32) + adapter).astype(bf16)
    q = q_ref[...]
    scores = [
        dot_nt(q, k_refs[j][...]) * score_scale + bias_ref[:, j * rows : (j + 1) * rows]
        for j in range(blocks)
    ]
    row_max = functools.reduce(jnp.maximum, [jnp.max(s, axis=1, keepdims=True) for s in scores])
    expo = [jnp.exp(s - row_max) for s in scores]
    total = functools.reduce(jnp.add, [jnp.sum(e, axis=1, keepdims=True) for e in expo])
    inverse = 1.0 / total
    prob = [e * inverse for e in expo]
    low = [p.astype(bf16) for p in prob]
    out = functools.reduce(jnp.add, [dot_nn(low[j], v_refs[j][...]) for j in range(blocks)])
    out = out.astype(bf16)
    grad = [dot_nt(cot, v_refs[j][...]) for j in range(blocks)]
    row_dot = functools.reduce(
        jnp.add, [jnp.sum(prob[j] * grad[j], axis=1, keepdims=True) for j in range(blocks)]
    )
    dscore = [(prob[j] * (grad[j] - row_dot)).astype(bf16) for j in range(blocks)]
    dq = functools.reduce(jnp.add, [dot_nn(dscore[j], k_refs[j][...]) for j in range(blocks)])
    dq_ref[...] = (dq * score_scale).astype(bf16)
    for j in range(blocks):
        target = own_ref if j == reach else back_refs[j]
        target[0] = (dot_tn(dscore[j], q) * score_scale).astype(target.dtype)
        target[1] = dot_tn(low[j], cot).astype(target.dtype)
    width = proj_ref.shape[2]
    slot = lax.broadcasted_iota(jnp.int32, (rows, width), 1) // PHM_N
    proj = jnp.where(slot == qinfo_ref[:, 1:2], dot_nt(out, lhi) + dot_nt(out, llo), 0.0)
    left = dot_tn(mix_hi, out) + dot_tn(mix_lo, out)

    @pl.when(part == 0)
    def _():
        proj_ref[0] = proj

    @pl.when(part != 0)
    def _():
        proj_ref[0] += proj

    @pl.when(block == 0)
    def _():
        left_ref[:, columns] = left

    @pl.when(block != 0)
    def _():
        left_ref[:, columns] += left


def attention(queries, frozen, keys, values, gate, qinfo, kdoc, rule, lhi, llo, block_count):
    rows, width = queries.shape
    local_heads = width // HEAD_DIM
    reach = len(keys) - 1
    heads_per_block = local_heads // block_count
    factor_columns = gate.shape[2]

    def per_head():
        return pl.BlockSpec((rows, HEAD_DIM), lambda h: (0, h))

    def pair():
        return pl.BlockSpec((2, rows, HEAD_DIM), lambda h: (0, 0, h))

    def whole(array):
        return pl.BlockSpec(array.shape, lambda h: (0,) * array.ndim)

    left_shape = jax.ShapeDtypeStruct(lhi.shape, f32)
    return pl.pallas_call(
        functools.partial(attention_kernel, reach, heads_per_block),
        grid=(local_heads,),
        in_specs=[per_head() for _ in range(2 + 2 * (reach + 1))]
        + [whole(a) for a in (gate, qinfo, kdoc, rule, lhi, llo)],
        out_specs=[per_head(), pair()]
        + [pair() for _ in range(reach)]
        + [
            pl.BlockSpec((1, rows, factor_columns), lambda h: (h // heads_per_block, 0, 0)),
            whole(left_shape),
        ],
        out_shape=[
            jax.ShapeDtypeStruct((rows, width), bf16),
            jax.ShapeDtypeStruct((2, rows, width), f32),
        ]
        + [jax.ShapeDtypeStruct((2, rows, width), bf16) for _ in range(reach)]
        + [jax.ShapeDtypeStruct((block_count, rows, factor_columns), f32), left_shape],
        scratch_shapes=[pltpu.VMEM((rows, (reach + 1) * rows), f32)],
        compiler_params=pltpu.CompilerParams(vmem_limit_bytes=32 * 2**20),
        cost_estimate=pl.CostEstimate(
            flops=12 * rows * rows * (reach + 1) * width,
            bytes_accessed=40 * rows * width,
            transcendentals=rows * rows * (reach + 1) * local_heads,
        ),
    )(queries, frozen, *keys, *values, gate, qinfo, kdoc, rule, lhi, llo)


def exchange_kernel(seq_count, head_count, x_ref, o_ref, landed, send_sem, recv_sem):
    count = seq_count * head_count
    me = lax.axis_index("seq") * head_count + lax.axis_index("head")

    def device(step):
        peer = lax.rem(me + step, count)
        return peer, {"seq": peer // head_count, "head": lax.rem(peer, head_count)}

    barrier = pltpu.get_barrier_semaphore()
    for step in range(1, count):
        pl.semaphore_signal(barrier, inc=1, device_id=device(step)[1], device_id_type=MESH)
    pl.semaphore_wait(barrier, count - 1)
    copies = []
    for step in range(1, count):
        peer, where = device(step)
        copy = pltpu.make_async_remote_copy(
            src_ref=x_ref.at[peer],
            dst_ref=landed.at[step],
            send_sem=send_sem.at[step],
            recv_sem=recv_sem.at[step],
            device_id=where,
            device_id_type=MESH,
        )
        copy.start()
        copies.append(copy)
    total = x_ref[me]
    for step in range(1, count):
        copies[step - 1].wait_recv()
        total = total + landed[step]
    o_ref[...] = total
    for copy in copies:
        copy.wait_send()


def exchange_sum(pieces, seq_count, head_count):
    count = seq_count * head_count
    return pl.pallas_call(
        functools.partial(exchange_kernel, seq_count, head_count),
        out_shape=jax.ShapeDtypeStruct(pieces.shape[1:], f32),
        in_specs=[pl.BlockSpec(memory_space=pltpu.VMEM)],
        out_specs=pl.BlockSpec(memory_space=pltpu.VMEM),
        scratch_shapes=[
            pltpu.VMEM(pieces.shape, f32),
            pltpu.SemaphoreType.DMA((count,)),
            pltpu.SemaphoreType.DMA((count,)),
        ],
        compiler_params=pltpu.CompilerParams(
            collective_id=0, has_side_effects=True, vmem_limit_bytes=32 * 2**20
        ),
        cost_estimate=pl.CostEstimate(
            flops=pieces.size, bytes_accessed=8 * pieces.size, transcendentals=0
        ),
    )(pieces)


def on_device(
    queries,
    key_vectors,
    value_vectors,
    frozen_grad,
    output_grad,
    document_ids,
    document_tenant,
    tenant_owner,
    phm_rule,
    phm_left,
    phm_right,
):
    rows = queries.shape[0]
    reach = (WINDOW + rows - 2) // rows
    seq_count = lax.axis_size("seq")
    head_count = lax.axis_size("head")
    seq_index = lax.axis_index("seq")
    head_index = lax.axis_index("head")
    tenants = tenant_owner.shape[0]
    block_count = PHM_N // head_count
    block_start = head_index * block_count
    factor_columns = tenants * PHM_N
    sub_left, sub_right = phm_left.shape[2], phm_right.shape[2]

    distances = list(range(reach, 0, -1))
    keys = [passed_along(key_vectors, "seq", d) for d in distances] + [key_vectors]
    values = [passed_along(value_vectors, "seq", d) for d in distances] + [value_vectors]

    slots = jnp.arange(tenants, dtype=jnp.int32)
    owner_hot = tenant_owner[None, :] == slots[:, None]

    def by_owner(array):
        hot = owner_hot.reshape((tenants, tenants) + (1,) * (array.ndim - 1))
        return jnp.sum(jnp.where(hot, array[None], 0.0), axis=1)

    rule = by_owner(phm_rule).reshape(factor_columns, PHM_N, PHM_N)
    left = by_owner(phm_left).reshape(factor_columns, sub_left)
    right = by_owner(phm_right).reshape(factor_columns, sub_right)

    lead = jnp.full((reach * rows,), -1, jnp.int32)
    key_docs = lax.dynamic_slice_in_dim(
        jnp.concatenate([lead, document_ids]), seq_index * rows, (reach + 1) * rows
    )
    query_docs = key_docs[reach * rows :]
    document_owner = jnp.sum(
        jnp.where(document_tenant[:, None] == slots[None, :], tenant_owner[None, :], 0), axis=1
    )
    documents = jnp.arange(document_tenant.shape[0], dtype=jnp.int32)
    token_owner = jnp.sum(
        jnp.where(query_docs[:, None] == documents[None, :], document_owner[None, :], 0), axis=1
    )
    qinfo = jnp.stack([query_docs, token_owner], axis=1)
    column_owner = jnp.arange(factor_columns, dtype=jnp.int32) // PHM_N
    token_mask = token_owner[:, None] == column_owner[None, :]

    shifted = jnp.concatenate(
        [
            jnp.pad(right, ((0, 0), (b * sub_right, (block_count - 1 - b) * sub_right)))
            for b in range(block_count)
        ],
        axis=0,
    )
    shifted_hi, shifted_lo = split_two(shifted)
    gate_both = dot_nt(output_grad, jnp.concatenate([shifted_hi, shifted_lo], axis=0))
    wide = block_count * factor_columns
    gate_sum = gate_both[:, :wide] + gate_both[:, wide:]
    gate_here = jnp.stack(
        [
            jnp.where(token_mask, gate_sum[:, b * factor_columns : (b + 1) * factor_columns], 0.0)
            for b in range(block_count)
        ]
    )
    gate = lax.all_gather(gate_here, "head", axis=0, tiled=True)

    rule_abc = rule.transpose(1, 2, 0)
    rule_rows = lax.dynamic_slice_in_dim(rule_abc, block_start, block_count, 0)
    rule_cols = lax.dynamic_slice_in_dim(rule_abc, block_start, block_count, 1)
    left_hi, left_lo = split_two(left)
    results = attention(
        queries, frozen_grad, keys, values, gate, qinfo, key_docs[None, :], rule_rows,
        left_hi, left_lo, block_count,
    )
    query_grad, own_terms = results[0], results[1]
    back = results[2 : 2 + reach]
    proj_here, left_sum = results[2 + reach :]
    returned = [passed_along(back[j], "seq", -(reach - j)) for j in range(reach)]

    proj = lax.all_gather(proj_here, "head", axis=0, tiled=True)
    rule_proj = jnp.sum(proj[:, None] * rule_cols[:, :, None, :], axis=0)
    rule_proj = jnp.concatenate([rule_proj[b] for b in range(block_count)], axis=1)
    proj_hi, proj_lo = split_two(rule_proj)
    right_both = dot_tn(jnp.concatenate([proj_hi, proj_lo], axis=1), output_grad)
    right_wide = right_both[:wide] + right_both[wide:]
    right_sum = sum(
        right_wide[
            b * factor_columns : (b + 1) * factor_columns, b * sub_right : (b + 1) * sub_right
        ]
        for b in range(block_count)
    )
    rule_here = jnp.sum(proj_here[:, None] * gate[None], axis=2)
    rule_sum = lax.dynamic_update_slice_in_dim(
        jnp.zeros((PHM_N, PHM_N, factor_columns), f32), rule_here, block_start, 0
    ).transpose(2, 0, 1)

    count = seq_count * head_count
    grad_scale = rows ** (-0.5)
    flat = jnp.concatenate(
        [
            right_sum.reshape(count, -1),
            left_sum.reshape(count, -1),
            rule_sum.reshape(count, -1),
        ],
        axis=1,
    )
    size = flat.shape[1]
    padded = -(-size // 1024) * 1024
    pieces = jnp.pad(flat * grad_scale, ((0, 0), (0, padded - size)))
    summed = exchange_sum(pieces.reshape(count, padded // 128, 128), seq_count, head_count)
    summed = summed.reshape(-1)
    factors = PHM_N // head_count
    right_end = factors * sub_right
    left_end = right_end + factors * sub_left
    right_grad = summed[:right_end].reshape(1, factors, sub_right)
    left_grad = summed[right_end:left_end].reshape(1, factors, sub_left)
    rule_grad = summed[left_end:size].reshape(1, factors, PHM_N, PHM_N)

    terms = own_terms
    for received in returned:
        terms = terms + received.astype(f32)
    key_grad = terms[0].astype(bf16)
    value_grad = terms[1].astype(bf16)
    return (query_grad, key_grad, value_grad, rule_grad, left_grad, right_grad)


def solution(mesh):
    rows = P(("groups", "seq"), "head")
    in_specs = (
        rows, rows, rows, rows, rows,
        P("groups"),
        P("groups"),
        P(),
        P("groups", None, None, None),
        P("groups", None, None),
        P("groups", None, None),
    )
    out_specs = (
        rows, rows, rows,
        P(("groups", "seq"), "head", None, None),
        P(("groups", "seq"), "head", None),
        P(("groups", "seq"), "head", None),
    )
    return jax.shard_map(
        on_device, mesh=mesh, in_specs=in_specs, out_specs=out_specs, check_vma=False
    )
```

```python
import functools

import jax
import jax.numpy as jnp
from jax import lax
from jax.experimental import pallas as pl
from jax.experimental.pallas import tpu as pltpu
from jax.sharding import PartitionSpec as P

HEAD_DIM = 128
WINDOW = 512
PHM_N = 4
MESH = pl.DeviceIdType.MESH

score_scale = 168.0 ** (-0.5)
neg_big = -1e30
f32 = jnp.float32
bf16 = jnp.bfloat16


def split_two(value):
    high = lax.reduce_precision(value, 8, 7)
    return high.astype(bf16), (value - high).astype(bf16)


def kernel_split(value):
    high = value.astype(bf16)
    return high, (value - high.astype(f32)).astype(bf16)


def dot_nt(a, b):
    return lax.dot_general(a, b, (((1,), (1,)), ((), ())), preferred_element_type=f32)


def dot_nn(a, b):
    return lax.dot_general(a, b, (((1,), (0,)), ((), ())), preferred_element_type=f32)


def dot_tn(a, b):
    return lax.dot_general(a, b, (((0,), (0,)), ((), ())), preferred_element_type=f32)


def main_kernel(reach, seq_count, head_count, *refs):
    (q_ref, k_ref, v_ref, frozen_ref, og_ref, gate_par_ref, qinfo_ref, kdoc_ref, rule_ref, lhi_ref, llo_ref,
     dq_ref, dk_ref, dv_ref, left_ref, right_ref, rule_out_ref,
     kv_land, back_out, back_land, own_ref, bias_ref, gate_ref, proj_ref,
     kv_send, kv_recv, back_send, back_recv, pair_send, pair_recv) = refs
    rows, width = q_ref.shape
    heads = width // HEAD_DIM
    blocks = reach + 1
    block_count = PHM_N // head_count
    heads_per_block = heads // block_count
    columns = gate_ref.shape[2]
    s = lax.axis_index("seq")
    me = lax.axis_index("head")
    mine = me * block_count
    distances = range(1, reach + 1)

    def span(h):
        return pl.ds(pl.multiple_of(h * HEAD_DIM, HEAD_DIM), HEAD_DIM)

    barrier = pltpu.get_barrier_semaphore()
    for d in distances:
        @pl.when(s + d < seq_count)
        def _():
            pl.semaphore_signal(barrier, inc=1, device_id={"seq": s + d}, device_id_type=MESH)

        @pl.when(s >= d)
        def _():
            pl.semaphore_signal(barrier, inc=1, device_id={"seq": s - d}, device_id_type=MESH)

    for step in range(1, head_count):
        pl.semaphore_signal(
            barrier, inc=1, device_id={"head": lax.rem(me + step, head_count)}, device_id_type=MESH
        )
    pl.semaphore_wait(
        barrier,
        jnp.minimum(s, reach) + jnp.minimum(seq_count - 1 - s, reach) + (head_count - 1),
    )

    def kv_copy(h, d, which):
        source = (k_ref, v_ref)[which]
        return pltpu.make_async_remote_copy(
            src_ref=source.at[:, span(h)],
            dst_ref=kv_land.at[d - 1, which, h],
            send_sem=kv_send.at[d - 1, which, h],
            recv_sem=kv_recv.at[d - 1, which, h],
            device_id={"seq": lax.rem(s + d, seq_count)},
            device_id_type=MESH,
        )

    def back_copy(h, d, which):
        return pltpu.make_async_remote_copy(
            src_ref=back_out.at[d - 1, which, h],
            dst_ref=back_land.at[d - 1, which, h],
            send_sem=back_send.at[d - 1, which, h],
            recv_sem=back_recv.at[d - 1, which, h],
            device_id={"seq": lax.rem(s - d + seq_count, seq_count)},
            device_id_type=MESH,
        )

    def pair_copy(buffer, index, step):
        return pltpu.make_async_remote_copy(
            src_ref=buffer.at[pl.ds(mine, block_count)],
            dst_ref=buffer.at[pl.ds(mine, block_count)],
            send_sem=pair_send.at[index, step],
            recv_sem=pair_recv.at[index, step],
            device_id={"head": lax.rem(me + step, head_count)},
            device_id_type=MESH,
        )

    def each(body):
        def step(h, carry):
            body(h)
            return carry

        lax.fori_loop(0, heads, step, 0)

    def for_pairs(condition, act):
        def body(h):
            for d in distances:
                @pl.when(condition(d))
                def _():
                    for which in range(2):
                        act(h, d, which)

        each(body)

    sends = lambda d: s + d < seq_count
    takes = lambda d: s >= d
    for_pairs(sends, lambda h, d, w: kv_copy(h, d, w).start())
    for d in distances:
        @pl.when(s < d)
        def _():
            kv_land[d - 1] = jnp.zeros(kv_land.shape[1:], bf16)

    slot = lax.broadcasted_iota(jnp.int32, (rows, columns), 1) // PHM_N
    mask = slot == qinfo_ref[:, 1:2]
    gate_both = dot_nt(og_ref[...], gate_par_ref[...])
    wide = block_count * columns
    for b in range(block_count):
        total = (
            gate_both[:, b * columns : (b + 1) * columns]
            + gate_both[:, wide + b * columns : wide + (b + 1) * columns]
        )
        gate_ref[mine + b] = jnp.where(mask, total, 0.0)
        proj_ref[mine + b] = jnp.zeros((rows, columns), f32)
    for step in range(1, head_count):
        pair_copy(gate_ref, 0, step).start()
    left_ref[...] = jnp.zeros_like(left_ref)
    query_pos = lax.broadcasted_iota(jnp.int32, (rows, rows), 0)
    key_pos = lax.broadcasted_iota(jnp.int32, (rows, rows), 1)
    for j in range(blocks):
        later = query_pos - key_pos + j * rows
        start = (reach - j) * rows
        same = qinfo_ref[:, 0:1] == kdoc_ref[:, start : start + rows]
        allowed = same & (later >= 0) & (later < WINDOW)
        bias_ref[j] = jnp.where(allowed, 0.0, neg_big)
    for step in range(1, head_count):
        pair_copy(gate_ref, 0, step).wait()

    def one_head(h):
        block = h // heads_per_block
        part_span = span(lax.rem(h, heads_per_block))
        mix = jnp.zeros((rows, columns), f32)
        for b in range(PHM_N):
            mix = mix + gate_ref[b] * rule_ref[mine + block, pl.ds(b, 1), :]
        mix_hi, mix_lo = kernel_split(mix)
        lhi = lhi_ref[:, part_span]
        llo = llo_ref[:, part_span]
        adapter = dot_nn(mix_hi, lhi) + dot_nn(mix_lo, lhi) + dot_nn(mix_hi, llo)
        cot = (frozen_ref[:, span(h)].astype(f32) + adapter).astype(bf16)
        q = q_ref[:, span(h)]
        for d in distances:
            @pl.when(takes(d))
            def _():
                for which in range(2):
                    kv_copy(h, d, which).wait_recv()

        keys = [k_ref[:, span(h)]] + [kv_land[d - 1, 0, h] for d in distances]
        values = [v_ref[:, span(h)]] + [kv_land[d - 1, 1, h] for d in distances]
        scores = [dot_nt(q, keys[j]) * score_scale + bias_ref[j] for j in range(blocks)]
        row_max = functools.reduce(jnp.maximum, [jnp.max(x, axis=1, keepdims=True) for x in scores])
        expo = [jnp.exp(x - row_max) for x in scores]
        total = functools.reduce(jnp.add, [jnp.sum(e, axis=1, keepdims=True) for e in expo])
        inverse = 1.0 / total
        prob = [e * inverse for e in expo]
        low = [p.astype(bf16) for p in prob]
        out = functools.reduce(jnp.add, [dot_nn(low[j], values[j]) for j in range(blocks)]).astype(bf16)
        grad = [dot_nt(cot, values[j]) for j in range(blocks)]
        row_dot = functools.reduce(
            jnp.add, [jnp.sum(prob[j] * grad[j], axis=1, keepdims=True) for j in range(blocks)]
        )
        dscore = [(prob[j] * (grad[j] - row_dot)).astype(bf16) for j in range(blocks)]
        for d in reversed(distances):
            back_out[d - 1, 0, h] = (dot_tn(dscore[d], q) * score_scale).astype(bf16)
            back_out[d - 1, 1, h] = dot_tn(low[d], cot).astype(bf16)

            @pl.when(takes(d))
            def _():
                for which in range(2):
                    back_copy(h, d, which).start()

        own_ref[0, h] = dot_tn(dscore[0], q) * score_scale
        own_ref[1, h] = dot_tn(low[0], cot)
        dq = functools.reduce(jnp.add, [dot_nn(dscore[j], keys[j]) for j in range(blocks)])
        dq_ref[:, span(h)] = (dq * score_scale).astype(bf16)
        proj = jnp.where(mask, dot_nt(out, lhi) + dot_nt(out, llo), 0.0)
        proj_ref[mine + block] += proj
        left_ref[:, part_span] += dot_tn(mix_hi, out) + dot_tn(mix_lo, out)

    each(one_head)

    for step in range(1, head_count):
        pair_copy(proj_ref, 1, step).start()
    for a in range(block_count):
        for b in range(PHM_N):
            rule_out_ref[a, b : b + 1, :] = jnp.sum(
                proj_ref[mine + a] * gate_ref[b], axis=0, keepdims=True
            )
    for step in range(1, head_count):
        pair_copy(proj_ref, 1, step).wait()
    for b in range(block_count):
        mixed = jnp.zeros((rows, columns), f32)
        for a in range(PHM_N):
            mixed = mixed + proj_ref[a] * rule_ref[a, pl.ds(mine + b, 1), :]
        high, low = kernel_split(mixed)
        og = og_ref[...]
        right_ref[b] = dot_tn(high, og) + dot_tn(low, og)

    def finish(h):
        for d in distances:
            @pl.when(sends(d))
            def _():
                for which in range(2):
                    back_copy(h, d, which).wait_recv()
                    own_ref[which, h] += back_land[d - 1, which, h].astype(f32)

        dk_ref[:, span(h)] = own_ref[0, h].astype(bf16)
        dv_ref[:, span(h)] = own_ref[1, h].astype(bf16)

    each(finish)
    for_pairs(sends, lambda h, d, w: kv_copy(h, d, w).wait_send())
    for_pairs(takes, lambda h, d, w: back_copy(h, d, w).wait_send())


def main_call(seq_count, head_count, reach, operands):
    queries, output_grad, lhi = operands[0], operands[4], operands[9]
    rows, width = queries.shape
    heads = width // HEAD_DIM
    columns = lhi.shape[0]
    block_count = PHM_N // head_count
    vmem = pl.BlockSpec(memory_space=pltpu.VMEM)
    wide = jax.ShapeDtypeStruct((rows, width), bf16)
    moved = (reach, 2, heads, rows, HEAD_DIM)
    dma = pltpu.SemaphoreType.DMA
    return pl.pallas_call(
        functools.partial(main_kernel, reach, seq_count, head_count),
        in_specs=[vmem] * len(operands),
        out_specs=[vmem] * 6,
        out_shape=[
            wide, wide, wide,
            jax.ShapeDtypeStruct(lhi.shape, f32),
            jax.ShapeDtypeStruct((block_count, columns, output_grad.shape[1]), f32),
            jax.ShapeDtypeStruct((block_count, PHM_N, columns), f32),
        ],
        scratch_shapes=[
            pltpu.VMEM(moved, bf16),
            pltpu.VMEM(moved, bf16),
            pltpu.VMEM(moved, bf16),
            pltpu.VMEM((2, heads, rows, HEAD_DIM), f32),
            pltpu.VMEM((reach + 1, rows, rows), f32),
            pltpu.VMEM((PHM_N, rows, columns), f32),
            pltpu.VMEM((PHM_N, rows, columns), f32),
            dma((reach, 2, heads)),
            dma((reach, 2, heads)),
            dma((reach, 2, heads)),
            dma((reach, 2, heads)),
            dma((2, head_count)),
            dma((2, head_count)),
        ],
        compiler_params=pltpu.CompilerParams(
            collective_id=1, has_side_effects=True, vmem_limit_bytes=48 * 2**20
        ),
    )(*operands)


def exchange_kernel(seq_count, head_count, x_ref, o_ref, landed, send_sem, recv_sem):
    count = seq_count * head_count
    me = lax.axis_index("seq") * head_count + lax.axis_index("head")

    def device(step):
        peer = lax.rem(me + step, count)
        return peer, {"seq": peer // head_count, "head": lax.rem(peer, head_count)}

    barrier = pltpu.get_barrier_semaphore()
    for step in range(1, count):
        pl.semaphore_signal(barrier, inc=1, device_id=device(step)[1], device_id_type=MESH)
    pl.semaphore_wait(barrier, count - 1)
    copies = []
    for step in range(1, count):
        peer, where = device(step)
        copy = pltpu.make_async_remote_copy(
            src_ref=x_ref.at[peer],
            dst_ref=landed.at[step],
            send_sem=send_sem.at[step],
            recv_sem=recv_sem.at[step],
            device_id=where,
            device_id_type=MESH,
        )
        copy.start()
        copies.append(copy)
    total = x_ref[me]
    for step in range(1, count):
        copies[step - 1].wait_recv()
        total = total + landed[step]
    o_ref[...] = total
    for copy in copies:
        copy.wait_send()


def exchange_sum(pieces, seq_count, head_count):
    count = seq_count * head_count
    return pl.pallas_call(
        functools.partial(exchange_kernel, seq_count, head_count),
        out_shape=jax.ShapeDtypeStruct(pieces.shape[1:], f32),
        in_specs=[pl.BlockSpec(memory_space=pltpu.VMEM)],
        out_specs=pl.BlockSpec(memory_space=pltpu.VMEM),
        scratch_shapes=[
            pltpu.VMEM(pieces.shape, f32),
            pltpu.SemaphoreType.DMA((count,)),
            pltpu.SemaphoreType.DMA((count,)),
        ],
        compiler_params=pltpu.CompilerParams(
            collective_id=0, has_side_effects=True, vmem_limit_bytes=32 * 2**20
        ),
        cost_estimate=pl.CostEstimate(
            flops=pieces.size, bytes_accessed=8 * pieces.size, transcendentals=0
        ),
    )(pieces)


def on_device(
    queries,
    key_vectors,
    value_vectors,
    frozen_grad,
    output_grad,
    document_ids,
    document_tenant,
    tenant_owner,
    phm_rule,
    phm_left,
    phm_right,
):
    rows = queries.shape[0]
    reach = (WINDOW + rows - 2) // rows
    seq_count = lax.axis_size("seq")
    head_count = lax.axis_size("head")
    seq_index = lax.axis_index("seq")
    head_index = lax.axis_index("head")
    tenants = tenant_owner.shape[0]
    block_count = PHM_N // head_count
    block_start = head_index * block_count
    factor_columns = tenants * PHM_N
    sub_left, sub_right = phm_left.shape[2], phm_right.shape[2]

    rule = phm_rule.transpose(2, 3, 0, 1).reshape(PHM_N, PHM_N, factor_columns)
    left = phm_left.reshape(factor_columns, sub_left)
    right = phm_right.reshape(factor_columns, sub_right)

    lead = jnp.full((reach * rows,), -1, jnp.int32)
    key_docs = lax.dynamic_slice_in_dim(
        jnp.concatenate([lead, document_ids]), seq_index * rows, (reach + 1) * rows
    )
    query_docs = key_docs[reach * rows :]
    documents = jnp.arange(document_tenant.shape[0], dtype=jnp.int32)
    token_tenant = jnp.sum(
        jnp.where(query_docs[:, None] == documents[None, :], document_tenant[None, :], 0), axis=1
    )
    qinfo = jnp.stack([query_docs, token_tenant], axis=1)

    shifted = jnp.concatenate(
        [
            jnp.pad(right, ((0, 0), (b * sub_right, (block_count - 1 - b) * sub_right)))
            for b in range(block_count)
        ],
        axis=0,
    )
    shifted_hi, shifted_lo = split_two(shifted)
    gate_params = jnp.concatenate([shifted_hi, shifted_lo], axis=0)
    left_hi, left_lo = split_two(left)
    query_grad, key_grad, value_grad, left_sum, right_both, rule_here = main_call(
        seq_count, head_count, reach,
        (queries, key_vectors, value_vectors, frozen_grad, output_grad, gate_params, qinfo,
         key_docs[None, :], rule, left_hi, left_lo),
    )
    right_sum = sum(
        right_both[b, :, b * sub_right : (b + 1) * sub_right] for b in range(block_count)
    )
    rule_sum = lax.dynamic_update_slice_in_dim(
        jnp.zeros((PHM_N, PHM_N, factor_columns), f32), rule_here, block_start, 0
    ).transpose(2, 0, 1)

    count = seq_count * head_count
    grad_scale = rows ** (-0.5)
    flat = jnp.concatenate(
        [
            right_sum.reshape(count, -1),
            left_sum.reshape(count, -1),
            rule_sum.reshape(count, -1),
        ],
        axis=1,
    )
    size = flat.shape[1]
    padded = -(-size // 1024) * 1024
    flat = jnp.pad(flat * grad_scale, ((0, 0), (0, padded - size)))
    slots = jnp.arange(tenants, dtype=jnp.int32)
    owner_hot = (tenant_owner[None, :] == slots[:, None])[:, :, None, None, None]
    rows_by_tenant = flat.reshape(1, tenants, head_count, padded // 128, 128)
    pieces = jnp.sum(jnp.where(owner_hot, rows_by_tenant, 0.0), axis=1)
    summed = exchange_sum(pieces.reshape(count, padded // 128, 128), seq_count, head_count)
    summed = summed.reshape(-1)
    factors = PHM_N // head_count
    right_end = factors * sub_right
    left_end = right_end + factors * sub_left
    right_grad = summed[:right_end].reshape(1, factors, sub_right)
    left_grad = summed[right_end:left_end].reshape(1, factors, sub_left)
    rule_grad = summed[left_end:size].reshape(1, factors, PHM_N, PHM_N)

    return (query_grad, key_grad, value_grad, rule_grad, left_grad, right_grad)


def solution(mesh):
    rows = P(("groups", "seq"), "head")
    in_specs = (
        rows, rows, rows, rows, rows,
        P("groups"),
        P("groups"),
        P(),
        P("groups", None, None, None),
        P("groups", None, None),
        P("groups", None, None),
    )
    out_specs = (
        rows, rows, rows,
        P(("groups", "seq"), "head", None, None),
        P(("groups", "seq"), "head", None),
        P(("groups", "seq"), "head", None),
    )
    return jax.shard_map(
        on_device, mesh=mesh, in_specs=in_specs, out_specs=out_specs, check_vma=False
    )
```

```python
import functools

import jax
import jax.numpy as jnp
from jax import lax
from jax.experimental import pallas as pl
from jax.experimental.pallas import tpu as pltpu
from jax.sharding import PartitionSpec as P

HEAD_DIM = 128
WINDOW = 512
PHM_N = 4
MESH = pl.DeviceIdType.MESH

score_scale = 168.0 ** (-0.5)
neg_big = -1e30
f32 = jnp.float32
bf16 = jnp.bfloat16


def split_two(value):
    high = lax.reduce_precision(value, 8, 7)
    return high.astype(bf16), (value - high).astype(bf16)


def kernel_split(value):
    high = value.astype(bf16)
    return high, (value - high.astype(f32)).astype(bf16)


def dot_nt(a, b):
    return lax.dot_general(a, b, (((1,), (1,)), ((), ())), preferred_element_type=f32)


def dot_nn(a, b):
    return lax.dot_general(a, b, (((1,), (0,)), ((), ())), preferred_element_type=f32)


def dot_tn(a, b):
    return lax.dot_general(a, b, (((0,), (0,)), ((), ())), preferred_element_type=f32)


def main_kernel(reach, seq_count, head_count, *refs):
    (q_ref, k_ref, v_ref, frozen_ref, og_ref, gate_par_ref, qinfo_ref, kdoc_ref, rule_ref, lhi_ref, llo_ref,
     dq_ref, dk_ref, dv_ref, left_ref, right_ref, rule_out_ref,
     kv_land, back_out, back_land, own_ref, bias_ref, gate_ref, proj_ref,
     kv_send, kv_recv, back_send, back_recv, pair_send, pair_recv) = refs
    rows, width = q_ref.shape
    heads = width // HEAD_DIM
    blocks = reach + 1
    block_count = PHM_N // head_count
    heads_per_block = heads // block_count
    columns = gate_ref.shape[2]
    s = lax.axis_index("seq")
    me = lax.axis_index("head")
    mine = me * block_count
    distances = range(1, reach + 1)
    relay = reach == 2 and seq_count % 2 == 0
    odd = lax.rem(s, 2) == 1
    relays = odd & (s >= 3)

    def span(h):
        return pl.ds(pl.multiple_of(h * HEAD_DIM, HEAD_DIM), HEAD_DIM)

    barrier = pltpu.get_barrier_semaphore()
    for d in distances:
        @pl.when(s + d < seq_count)
        def _():
            pl.semaphore_signal(barrier, inc=1, device_id={"seq": s + d}, device_id_type=MESH)

        @pl.when(s >= d)
        def _():
            pl.semaphore_signal(barrier, inc=1, device_id={"seq": s - d}, device_id_type=MESH)

    for step in range(1, head_count):
        pl.semaphore_signal(
            barrier, inc=1, device_id={"head": lax.rem(me + step, head_count)}, device_id_type=MESH
        )
    pl.semaphore_wait(
        barrier,
        jnp.minimum(s, reach) + jnp.minimum(seq_count - 1 - s, reach) + (head_count - 1),
    )

    def kv_copy(h, d, which):
        source = (k_ref, v_ref)[which]
        return pltpu.make_async_remote_copy(
            src_ref=source.at[:, span(h)],
            dst_ref=kv_land.at[d - 1, which, h],
            send_sem=kv_send.at[d - 1, which, h],
            recv_sem=kv_recv.at[d - 1, which, h],
            device_id={"seq": lax.rem(s + d, seq_count)},
            device_id_type=MESH,
        )

    def back_target(d):
        direct = lax.rem(s - d + seq_count, seq_count)
        return jnp.where(odd, direct, lax.rem(s + 1, seq_count)) if relay and d == 1 else direct

    def forward_copy(h, which):
        return pltpu.make_async_remote_copy(
            src_ref=kv_land.at[1, which, h],
            dst_ref=kv_land.at[0, which, h],
            send_sem=kv_send.at[0, which, h],
            recv_sem=kv_recv.at[0, which, h],
            device_id={"seq": lax.rem(s - 1 + seq_count, seq_count)},
            device_id_type=MESH,
        )

    def back_copy(h, d, which):
        return pltpu.make_async_remote_copy(
            src_ref=back_out.at[d - 1, which, h],
            dst_ref=back_land.at[d - 1, which, h],
            send_sem=back_send.at[d - 1, which, h],
            recv_sem=back_recv.at[d - 1, which, h],
            device_id={"seq": back_target(d)},
            device_id_type=MESH,
        )

    def pair_copy(buffer, index, step):
        return pltpu.make_async_remote_copy(
            src_ref=buffer.at[pl.ds(mine, block_count)],
            dst_ref=buffer.at[pl.ds(mine, block_count)],
            send_sem=pair_send.at[index, step],
            recv_sem=pair_recv.at[index, step],
            device_id={"head": lax.rem(me + step, head_count)},
            device_id_type=MESH,
        )

    def each(body):
        def step(h, carry):
            body(h)
            return carry

        lax.fori_loop(0, heads, step, 0)

    def for_pairs(condition, act):
        def body(h):
            for d in distances:
                @pl.when(condition(d))
                def _():
                    for which in range(2):
                        act(h, d, which)

        each(body)

    def sends(d):
        return ~odd if relay and d == 1 else s + d < seq_count

    def relay_back(h):
        for which in range(2):
            back_copy(h, 1, which).wait_recv()
            joined = back_out[1, which, h].astype(f32) + back_land[0, which, h].astype(f32)
            back_out[1, which, h] = joined.astype(bf16)
            back_copy(h, 2, which).start()

    takes = lambda d: s >= d
    for_pairs(sends, lambda h, d, w: kv_copy(h, d, w).start())
    for d in distances:
        @pl.when(s < d)
        def _():
            kv_land[d - 1] = jnp.zeros(kv_land.shape[1:], bf16)

    slot = lax.broadcasted_iota(jnp.int32, (rows, columns), 1) // PHM_N
    mask = slot == qinfo_ref[:, 1:2]
    gate_both = dot_nt(og_ref[...], gate_par_ref[...])
    wide = block_count * columns
    for b in range(block_count):
        total = (
            gate_both[:, b * columns : (b + 1) * columns]
            + gate_both[:, wide + b * columns : wide + (b + 1) * columns]
        )
        gate_ref[mine + b] = jnp.where(mask, total, 0.0)
        proj_ref[mine + b] = jnp.zeros((rows, columns), f32)
    for step in range(1, head_count):
        pair_copy(gate_ref, 0, step).start()
    left_ref[...] = jnp.zeros_like(left_ref)
    query_pos = lax.broadcasted_iota(jnp.int32, (rows, rows), 0)
    key_pos = lax.broadcasted_iota(jnp.int32, (rows, rows), 1)
    for j in range(blocks):
        later = query_pos - key_pos + j * rows
        start = (reach - j) * rows
        same = qinfo_ref[:, 0:1] == kdoc_ref[:, start : start + rows]
        allowed = same & (later >= 0) & (later < WINDOW)
        bias_ref[j] = jnp.where(allowed, 0.0, neg_big)
    for step in range(1, head_count):
        pair_copy(gate_ref, 0, step).wait()

    def one_head(h):
        block = h // heads_per_block
        part_span = span(lax.rem(h, heads_per_block))
        mix = jnp.zeros((rows, columns), f32)
        for b in range(PHM_N):
            mix = mix + gate_ref[b] * rule_ref[mine + block, pl.ds(b, 1), :]
        mix_hi, mix_lo = kernel_split(mix)
        lhi = lhi_ref[:, part_span]
        llo = llo_ref[:, part_span]
        adapter = dot_nn(mix_hi, lhi) + dot_nn(mix_lo, lhi) + dot_nn(mix_hi, llo)
        cot = (frozen_ref[:, span(h)].astype(f32) + adapter).astype(bf16)
        q = q_ref[:, span(h)]
        for d in reversed(distances):
            @pl.when(takes(d))
            def _():
                for which in range(2):
                    kv_copy(h, d, which).wait_recv()

            if relay and d == 2:
                @pl.when(relays)
                def _():
                    for which in range(2):
                        forward_copy(h, which).start()

        keys = [k_ref[:, span(h)]] + [kv_land[d - 1, 0, h] for d in distances]
        values = [v_ref[:, span(h)]] + [kv_land[d - 1, 1, h] for d in distances]
        scores = [dot_nt(q, keys[j]) * score_scale + bias_ref[j] for j in range(blocks)]
        row_max = functools.reduce(jnp.maximum, [jnp.max(x, axis=1, keepdims=True) for x in scores])
        expo = [jnp.exp(x - row_max) for x in scores]
        total = functools.reduce(jnp.add, [jnp.sum(e, axis=1, keepdims=True) for e in expo])
        inverse = 1.0 / total
        prob = [e * inverse for e in expo]
        low = [p.astype(bf16) for p in prob]
        out = functools.reduce(jnp.add, [dot_nn(low[j], values[j]) for j in range(blocks)]).astype(bf16)
        grad = [dot_nt(cot, values[j]) for j in range(blocks)]
        row_dot = functools.reduce(
            jnp.add, [jnp.sum(prob[j] * grad[j], axis=1, keepdims=True) for j in range(blocks)]
        )
        dscore = [(prob[j] * (grad[j] - row_dot)).astype(bf16) for j in range(blocks)]
        for d in reversed(distances):
            back_out[d - 1, 0, h] = (dot_tn(dscore[d], q) * score_scale).astype(bf16)
            back_out[d - 1, 1, h] = dot_tn(low[d], cot).astype(bf16)

            @pl.when(takes(d) & ~odd if relay and d == 2 else takes(d))
            def _():
                for which in range(2):
                    back_copy(h, d, which).start()

        own_ref[0, h] = dot_tn(dscore[0], q) * score_scale
        own_ref[1, h] = dot_tn(low[0], cot)
        dq = functools.reduce(jnp.add, [dot_nn(dscore[j], keys[j]) for j in range(blocks)])
        dq_ref[:, span(h)] = (dq * score_scale).astype(bf16)
        proj = jnp.where(mask, dot_nt(out, lhi) + dot_nt(out, llo), 0.0)
        proj_ref[mine + block] += proj
        left_ref[:, part_span] += dot_tn(mix_hi, out) + dot_tn(mix_lo, out)

        if relay:
            @pl.when(relays & (h >= 2))
            def _():
                relay_back(jnp.maximum(h - 2, 0))

    each(one_head)
    if relay:
        @pl.when(relays)
        def _():
            for h in range(max(0, heads - 2), heads):
                relay_back(h)

    for step in range(1, head_count):
        pair_copy(proj_ref, 1, step).start()
    for a in range(block_count):
        for b in range(PHM_N):
            rule_out_ref[a, b : b + 1, :] = jnp.sum(
                proj_ref[mine + a] * gate_ref[b], axis=0, keepdims=True
            )
    for step in range(1, head_count):
        pair_copy(proj_ref, 1, step).wait()
    for b in range(block_count):
        mixed = jnp.zeros((rows, columns), f32)
        for a in range(PHM_N):
            mixed = mixed + proj_ref[a] * rule_ref[a, pl.ds(mine + b, 1), :]
        high, low = kernel_split(mixed)
        og = og_ref[...]
        right_ref[b] = dot_tn(high, og) + dot_tn(low, og)

    def finish(h):
        for d in distances:
            @pl.when(sends(d))
            def _():
                for which in range(2):
                    back_copy(h, d, which).wait_recv()
                    own_ref[which, h] += back_land[d - 1, which, h].astype(f32)

        dk_ref[:, span(h)] = own_ref[0, h].astype(bf16)
        dv_ref[:, span(h)] = own_ref[1, h].astype(bf16)

    each(finish)
    for_pairs(sends, lambda h, d, w: kv_copy(h, d, w).wait_send())
    for_pairs(takes, lambda h, d, w: back_copy(h, d, w).wait_send())
    if relay:
        @pl.when(relays)
        def _():
            each(lambda h: [forward_copy(h, w).wait_send() for w in range(2)])


def main_call(seq_count, head_count, reach, operands):
    queries, output_grad, lhi = operands[0], operands[4], operands[9]
    rows, width = queries.shape
    heads = width // HEAD_DIM
    columns = lhi.shape[0]
    block_count = PHM_N // head_count
    vmem = pl.BlockSpec(memory_space=pltpu.VMEM)
    wide = jax.ShapeDtypeStruct((rows, width), bf16)
    moved = (reach, 2, heads, rows, HEAD_DIM)
    dma = pltpu.SemaphoreType.DMA
    return pl.pallas_call(
        functools.partial(main_kernel, reach, seq_count, head_count),
        in_specs=[vmem] * len(operands),
        out_specs=[vmem] * 6,
        out_shape=[
            wide, wide, wide,
            jax.ShapeDtypeStruct(lhi.shape, f32),
            jax.ShapeDtypeStruct((block_count, columns, output_grad.shape[1]), f32),
            jax.ShapeDtypeStruct((block_count, PHM_N, columns), f32),
        ],
        scratch_shapes=[
            pltpu.VMEM(moved, bf16),
            pltpu.VMEM(moved, bf16),
            pltpu.VMEM(moved, bf16),
            pltpu.VMEM((2, heads, rows, HEAD_DIM), f32),
            pltpu.VMEM((reach + 1, rows, rows), f32),
            pltpu.VMEM((PHM_N, rows, columns), f32),
            pltpu.VMEM((PHM_N, rows, columns), f32),
            dma((reach, 2, heads)),
            dma((reach, 2, heads)),
            dma((reach, 2, heads)),
            dma((reach, 2, heads)),
            dma((2, head_count)),
            dma((2, head_count)),
        ],
        compiler_params=pltpu.CompilerParams(
            collective_id=1, has_side_effects=True, vmem_limit_bytes=48 * 2**20
        ),
    )(*operands)


def exchange_kernel(seq_count, head_count, x_ref, o_ref, landed, send_sem, recv_sem):
    count = seq_count * head_count
    me = lax.axis_index("seq") * head_count + lax.axis_index("head")

    def device(step):
        peer = lax.rem(me + step, count)
        return peer, {"seq": peer // head_count, "head": lax.rem(peer, head_count)}

    barrier = pltpu.get_barrier_semaphore()
    for step in range(1, count):
        pl.semaphore_signal(barrier, inc=1, device_id=device(step)[1], device_id_type=MESH)
    pl.semaphore_wait(barrier, count - 1)
    copies = []
    for step in range(1, count):
        peer, where = device(step)
        copy = pltpu.make_async_remote_copy(
            src_ref=x_ref.at[peer],
            dst_ref=landed.at[step],
            send_sem=send_sem.at[step],
            recv_sem=recv_sem.at[step],
            device_id=where,
            device_id_type=MESH,
        )
        copy.start()
        copies.append(copy)
    total = x_ref[me]
    for step in range(1, count):
        copies[step - 1].wait_recv()
        total = total + landed[step]
    o_ref[...] = total
    for copy in copies:
        copy.wait_send()


def exchange_sum(pieces, seq_count, head_count):
    count = seq_count * head_count
    return pl.pallas_call(
        functools.partial(exchange_kernel, seq_count, head_count),
        out_shape=jax.ShapeDtypeStruct(pieces.shape[1:], f32),
        in_specs=[pl.BlockSpec(memory_space=pltpu.VMEM)],
        out_specs=pl.BlockSpec(memory_space=pltpu.VMEM),
        scratch_shapes=[
            pltpu.VMEM(pieces.shape, f32),
            pltpu.SemaphoreType.DMA((count,)),
            pltpu.SemaphoreType.DMA((count,)),
        ],
        compiler_params=pltpu.CompilerParams(
            collective_id=0, has_side_effects=True, vmem_limit_bytes=32 * 2**20
        ),
        cost_estimate=pl.CostEstimate(
            flops=pieces.size, bytes_accessed=8 * pieces.size, transcendentals=0
        ),
    )(pieces)


def on_device(
    queries,
    key_vectors,
    value_vectors,
    frozen_grad,
    output_grad,
    document_ids,
    document_tenant,
    tenant_owner,
    phm_rule,
    phm_left,
    phm_right,
):
    rows = queries.shape[0]
    reach = (WINDOW + rows - 2) // rows
    seq_count = lax.axis_size("seq")
    head_count = lax.axis_size("head")
    seq_index = lax.axis_index("seq")
    head_index = lax.axis_index("head")
    tenants = tenant_owner.shape[0]
    block_count = PHM_N // head_count
    block_start = head_index * block_count
    factor_columns = tenants * PHM_N
    sub_left, sub_right = phm_left.shape[2], phm_right.shape[2]

    rule = phm_rule.transpose(2, 3, 0, 1).reshape(PHM_N, PHM_N, factor_columns)
    left = phm_left.reshape(factor_columns, sub_left)
    right = phm_right.reshape(factor_columns, sub_right)

    lead = jnp.full((reach * rows,), -1, jnp.int32)
    key_docs = lax.dynamic_slice_in_dim(
        jnp.concatenate([lead, document_ids]), seq_index * rows, (reach + 1) * rows
    )
    query_docs = key_docs[reach * rows :]
    documents = jnp.arange(document_tenant.shape[0], dtype=jnp.int32)
    token_tenant = jnp.sum(
        jnp.where(query_docs[:, None] == documents[None, :], document_tenant[None, :], 0), axis=1
    )
    qinfo = jnp.stack([query_docs, token_tenant], axis=1)

    shifted = jnp.concatenate(
        [
            jnp.pad(right, ((0, 0), (b * sub_right, (block_count - 1 - b) * sub_right)))
            for b in range(block_count)
        ],
        axis=0,
    )
    shifted_hi, shifted_lo = split_two(shifted)
    gate_params = jnp.concatenate([shifted_hi, shifted_lo], axis=0)
    left_hi, left_lo = split_two(left)
    query_grad, key_grad, value_grad, left_sum, right_both, rule_here = main_call(
        seq_count, head_count, reach,
        (queries, key_vectors, value_vectors, frozen_grad, output_grad, gate_params, qinfo,
         key_docs[None, :], rule, left_hi, left_lo),
    )
    right_sum = sum(
        right_both[b, :, b * sub_right : (b + 1) * sub_right] for b in range(block_count)
    )
    rule_sum = lax.dynamic_update_slice_in_dim(
        jnp.zeros((PHM_N, PHM_N, factor_columns), f32), rule_here, block_start, 0
    ).transpose(2, 0, 1)

    count = seq_count * head_count
    grad_scale = rows ** (-0.5)
    flat = jnp.concatenate(
        [
            right_sum.reshape(count, -1),
            left_sum.reshape(count, -1),
            rule_sum.reshape(count, -1),
        ],
        axis=1,
    )
    size = flat.shape[1]
    padded = -(-size // 1024) * 1024
    flat = jnp.pad(flat * grad_scale, ((0, 0), (0, padded - size)))
    slots = jnp.arange(tenants, dtype=jnp.int32)
    owner_hot = (tenant_owner[None, :] == slots[:, None])[:, :, None, None, None]
    rows_by_tenant = flat.reshape(1, tenants, head_count, padded // 128, 128)
    pieces = jnp.sum(jnp.where(owner_hot, rows_by_tenant, 0.0), axis=1)
    summed = exchange_sum(pieces.reshape(count, padded // 128, 128), seq_count, head_count)
    summed = summed.reshape(-1)
    factors = PHM_N // head_count
    right_end = factors * sub_right
    left_end = right_end + factors * sub_left
    right_grad = summed[:right_end].reshape(1, factors, sub_right)
    left_grad = summed[right_end:left_end].reshape(1, factors, sub_left)
    rule_grad = summed[left_end:size].reshape(1, factors, PHM_N, PHM_N)

    return (query_grad, key_grad, value_grad, rule_grad, left_grad, right_grad)


def solution(mesh):
    rows = P(("groups", "seq"), "head")
    in_specs = (
        rows, rows, rows, rows, rows,
        P("groups"),
        P("groups"),
        P(),
        P("groups", None, None, None),
        P("groups", None, None),
        P("groups", None, None),
    )
    out_specs = (
        rows, rows, rows,
        P(("groups", "seq"), "head", None, None),
        P(("groups", "seq"), "head", None),
        P(("groups", "seq"), "head", None),
    )
    return jax.shard_map(
        on_device, mesh=mesh, in_specs=in_specs, out_specs=out_specs, check_vma=False
    )
```

```python
import functools

import jax
import jax.numpy as jnp
from jax import lax
from jax.experimental import pallas as pl
from jax.experimental.pallas import tpu as pltpu
from jax.sharding import PartitionSpec as P

HEAD_DIM = 128
WINDOW = 512
PHM_N = 4
MESH = pl.DeviceIdType.MESH

score_scale = 168.0 ** (-0.5)
neg_big = -1e30
f32 = jnp.float32
bf16 = jnp.bfloat16


def split_two(value):
    high = lax.reduce_precision(value, 8, 7)
    return high.astype(bf16), (value - high).astype(bf16)


def kernel_split(value):
    high = value.astype(bf16)
    return high, (value - high.astype(f32)).astype(bf16)


def dot_nt(a, b):
    return lax.dot_general(a, b, (((1,), (1,)), ((), ())), preferred_element_type=f32)


def dot_nn(a, b):
    return lax.dot_general(a, b, (((1,), (0,)), ((), ())), preferred_element_type=f32)


def dot_tn(a, b):
    return lax.dot_general(a, b, (((0,), (0,)), ((), ())), preferred_element_type=f32)


def main_kernel(reach, seq_count, head_count, *refs):
    (q_ref, k_ref, v_ref, frozen_ref, og_ref, gate_par_ref, qinfo_ref, kdoc_ref, rule_ref, lhi_ref, llo_ref,
     dq_ref, dk_ref, dv_ref, left_ref, right_ref, rule_out_ref,
     kv_land, back_out, back_land, own_ref, bias_ref, gate_ref, proj_ref,
     kv_send, kv_recv, back_send, back_recv, pair_send, pair_recv) = refs
    rows, width = q_ref.shape
    heads = width // HEAD_DIM
    blocks = reach + 1
    block_count = PHM_N // head_count
    heads_per_block = heads // block_count
    columns = gate_ref.shape[2]
    s = lax.axis_index("seq")
    me = lax.axis_index("head")
    mine = me * block_count
    distances = range(1, reach + 1)

    def span(h):
        return pl.ds(pl.multiple_of(h * HEAD_DIM, HEAD_DIM), HEAD_DIM)

    barrier = pltpu.get_barrier_semaphore()
    for d in distances:
        @pl.when(s + d < seq_count)
        def _():
            pl.semaphore_signal(barrier, inc=1, device_id={"seq": s + d}, device_id_type=MESH)

        @pl.when(s >= d)
        def _():
            pl.semaphore_signal(barrier, inc=1, device_id={"seq": s - d}, device_id_type=MESH)

    for step in range(1, head_count):
        pl.semaphore_signal(
            barrier, inc=1, device_id={"head": lax.rem(me + step, head_count)}, device_id_type=MESH
        )
    pl.semaphore_wait(
        barrier,
        jnp.minimum(s, reach) + jnp.minimum(seq_count - 1 - s, reach) + (head_count - 1),
    )

    def kv_copy(h, d, which):
        source = (k_ref, v_ref)[which]
        return pltpu.make_async_remote_copy(
            src_ref=source.at[:, span(h)],
            dst_ref=kv_land.at[d - 1, which, h],
            send_sem=kv_send.at[d - 1, which, h],
            recv_sem=kv_recv.at[d - 1, which, h],
            device_id={"seq": lax.rem(s + d, seq_count)},
            device_id_type=MESH,
        )

    def back_copy(h, d, which):
        return pltpu.make_async_remote_copy(
            src_ref=back_out.at[d - 1, which, h],
            dst_ref=back_land.at[d - 1, which, h],
            send_sem=back_send.at[d - 1, which, h],
            recv_sem=back_recv.at[d - 1, which, h],
            device_id={"seq": lax.rem(s - d + seq_count, seq_count)},
            device_id_type=MESH,
        )

    def pair_copy(buffer, index, step):
        return pltpu.make_async_remote_copy(
            src_ref=buffer.at[pl.ds(mine, block_count)],
            dst_ref=buffer.at[pl.ds(mine, block_count)],
            send_sem=pair_send.at[index, step],
            recv_sem=pair_recv.at[index, step],
            device_id={"head": lax.rem(me + step, head_count)},
            device_id_type=MESH,
        )

    def each(body):
        def step(h, carry):
            body(h)
            return carry

        lax.fori_loop(0, heads, step, 0)

    def for_pairs(condition, act):
        def body(h):
            for d in reversed(distances):
                @pl.when(condition(d))
                def _():
                    for which in range(2):
                        act(h, d, which)

        each(body)

    sends = lambda d: s + d < seq_count
    takes = lambda d: s >= d
    for_pairs(sends, lambda h, d, w: kv_copy(h, d, w).start())
    for d in distances:
        @pl.when(s < d)
        def _():
            kv_land[d - 1] = jnp.zeros(kv_land.shape[1:], bf16)

    slot = lax.broadcasted_iota(jnp.int32, (rows, columns), 1) // PHM_N
    mask = slot == qinfo_ref[:, 1:2]
    gate_both = dot_nt(og_ref[...], gate_par_ref[...])
    wide = block_count * columns
    for b in range(block_count):
        total = (
            gate_both[:, b * columns : (b + 1) * columns]
            + gate_both[:, wide + b * columns : wide + (b + 1) * columns]
        )
        gate_ref[mine + b] = jnp.where(mask, total, 0.0)
        proj_ref[mine + b] = jnp.zeros((rows, columns), f32)
    for step in range(1, head_count):
        pair_copy(gate_ref, 0, step).start()
    left_ref[...] = jnp.zeros_like(left_ref)
    query_pos = lax.broadcasted_iota(jnp.int32, (rows, rows), 0)
    key_pos = lax.broadcasted_iota(jnp.int32, (rows, rows), 1)
    for j in range(blocks):
        later = query_pos - key_pos + j * rows
        start = (reach - j) * rows
        same = qinfo_ref[:, 0:1] == kdoc_ref[:, start : start + rows]
        allowed = same & (later >= 0) & (later < WINDOW)
        bias_ref[j] = jnp.where(allowed, 0.0, neg_big)
    for step in range(1, head_count):
        pair_copy(gate_ref, 0, step).wait()

    def one_head(h):
        block = h // heads_per_block
        part_span = span(lax.rem(h, heads_per_block))
        mix = jnp.zeros((rows, columns), f32)
        for b in range(PHM_N):
            mix = mix + gate_ref[b] * rule_ref[mine + block, pl.ds(b, 1), :]
        mix_hi, mix_lo = kernel_split(mix)
        lhi = lhi_ref[:, part_span]
        llo = llo_ref[:, part_span]
        adapter = dot_nn(mix_hi, lhi) + dot_nn(mix_lo, lhi) + dot_nn(mix_hi, llo)
        cot = (frozen_ref[:, span(h)].astype(f32) + adapter).astype(bf16)
        q = q_ref[:, span(h)]
        for d in distances:
            @pl.when(takes(d))
            def _():
                for which in range(2):
                    kv_copy(h, d, which).wait_recv()

        keys = [k_ref[:, span(h)]] + [kv_land[d - 1, 0, h] for d in distances]
        values = [v_ref[:, span(h)]] + [kv_land[d - 1, 1, h] for d in distances]
        scores = [dot_nt(q, keys[j]) * score_scale + bias_ref[j] for j in range(blocks)]
        row_max = functools.reduce(jnp.maximum, [jnp.max(x, axis=1, keepdims=True) for x in scores])
        expo = [jnp.exp(x - row_max) for x in scores]
        total = functools.reduce(jnp.add, [jnp.sum(e, axis=1, keepdims=True) for e in expo])
        inverse = 1.0 / total
        prob = [e * inverse for e in expo]
        low = [p.astype(bf16) for p in prob]
        out = functools.reduce(jnp.add, [dot_nn(low[j], values[j]) for j in range(blocks)]).astype(bf16)
        grad = [dot_nt(cot, values[j]) for j in range(blocks)]
        row_dot = functools.reduce(
            jnp.add, [jnp.sum(prob[j] * grad[j], axis=1, keepdims=True) for j in range(blocks)]
        )
        dscore = [(prob[j] * (grad[j] - row_dot)).astype(bf16) for j in range(blocks)]
        for d in reversed(distances):
            back_out[d - 1, 0, h] = (dot_tn(dscore[d], q) * score_scale).astype(bf16)
            back_out[d - 1, 1, h] = dot_tn(low[d], cot).astype(bf16)

            @pl.when(takes(d))
            def _():
                for which in range(2):
                    back_copy(h, d, which).start()

        own_ref[0, h] = dot_tn(dscore[0], q) * score_scale
        own_ref[1, h] = dot_tn(low[0], cot)
        dq = functools.reduce(jnp.add, [dot_nn(dscore[j], keys[j]) for j in range(blocks)])
        dq_ref[:, span(h)] = (dq * score_scale).astype(bf16)
        proj = jnp.where(mask, dot_nt(out, lhi) + dot_nt(out, llo), 0.0)
        proj_ref[mine + block] += proj
        left_ref[:, part_span] += dot_tn(mix_hi, out) + dot_tn(mix_lo, out)

    each(one_head)

    for step in range(1, head_count):
        pair_copy(proj_ref, 1, step).start()
    for a in range(block_count):
        for b in range(PHM_N):
            rule_out_ref[a, b : b + 1, :] = jnp.sum(
                proj_ref[mine + a] * gate_ref[b], axis=0, keepdims=True
            )
    for step in range(1, head_count):
        pair_copy(proj_ref, 1, step).wait()
    for b in range(block_count):
        mixed = jnp.zeros((rows, columns), f32)
        for a in range(PHM_N):
            mixed = mixed + proj_ref[a] * rule_ref[a, pl.ds(mine + b, 1), :]
        high, low = kernel_split(mixed)
        og = og_ref[...]
        right_ref[b] = dot_tn(high, og) + dot_tn(low, og)

    def finish(h):
        for d in distances:
            @pl.when(sends(d))
            def _():
                for which in range(2):
                    back_copy(h, d, which).wait_recv()
                    own_ref[which, h] += back_land[d - 1, which, h].astype(f32)

        dk_ref[:, span(h)] = own_ref[0, h].astype(bf16)
        dv_ref[:, span(h)] = own_ref[1, h].astype(bf16)

    each(finish)
    for_pairs(sends, lambda h, d, w: kv_copy(h, d, w).wait_send())
    for_pairs(takes, lambda h, d, w: back_copy(h, d, w).wait_send())


def main_call(seq_count, head_count, reach, operands):
    queries, output_grad, lhi = operands[0], operands[4], operands[9]
    rows, width = queries.shape
    heads = width // HEAD_DIM
    columns = lhi.shape[0]
    block_count = PHM_N // head_count
    vmem = pl.BlockSpec(memory_space=pltpu.VMEM)
    wide = jax.ShapeDtypeStruct((rows, width), bf16)
    moved = (reach, 2, heads, rows, HEAD_DIM)
    dma = pltpu.SemaphoreType.DMA
    return pl.pallas_call(
        functools.partial(main_kernel, reach, seq_count, head_count),
        in_specs=[vmem] * len(operands),
        out_specs=[vmem] * 6,
        out_shape=[
            wide, wide, wide,
            jax.ShapeDtypeStruct(lhi.shape, f32),
            jax.ShapeDtypeStruct((block_count, columns, output_grad.shape[1]), f32),
            jax.ShapeDtypeStruct((block_count, PHM_N, columns), f32),
        ],
        scratch_shapes=[
            pltpu.VMEM(moved, bf16),
            pltpu.VMEM(moved, bf16),
            pltpu.VMEM(moved, bf16),
            pltpu.VMEM((2, heads, rows, HEAD_DIM), f32),
            pltpu.VMEM((reach + 1, rows, rows), f32),
            pltpu.VMEM((PHM_N, rows, columns), f32),
            pltpu.VMEM((PHM_N, rows, columns), f32),
            dma((reach, 2, heads)),
            dma((reach, 2, heads)),
            dma((reach, 2, heads)),
            dma((reach, 2, heads)),
            dma((2, head_count)),
            dma((2, head_count)),
        ],
        compiler_params=pltpu.CompilerParams(
            collective_id=1, has_side_effects=True, vmem_limit_bytes=48 * 2**20
        ),
    )(*operands)


def exchange_kernel(seq_count, head_count, x_ref, o_ref, landed, send_sem, recv_sem):
    count = seq_count * head_count
    me = lax.axis_index("seq") * head_count + lax.axis_index("head")

    def device(step):
        peer = lax.rem(me + step, count)
        return peer, {"seq": peer // head_count, "head": lax.rem(peer, head_count)}

    barrier = pltpu.get_barrier_semaphore()
    for step in range(1, count):
        pl.semaphore_signal(barrier, inc=1, device_id=device(step)[1], device_id_type=MESH)
    pl.semaphore_wait(barrier, count - 1)
    copies = []
    for step in range(1, count):
        peer, where = device(step)
        copy = pltpu.make_async_remote_copy(
            src_ref=x_ref.at[peer],
            dst_ref=landed.at[step],
            send_sem=send_sem.at[step],
            recv_sem=recv_sem.at[step],
            device_id=where,
            device_id_type=MESH,
        )
        copy.start()
        copies.append(copy)
    total = x_ref[me]
    for step in range(1, count):
        copies[step - 1].wait_recv()
        total = total + landed[step]
    o_ref[...] = total
    for copy in copies:
        copy.wait_send()


def exchange_sum(pieces, seq_count, head_count):
    count = seq_count * head_count
    return pl.pallas_call(
        functools.partial(exchange_kernel, seq_count, head_count),
        out_shape=jax.ShapeDtypeStruct(pieces.shape[1:], f32),
        in_specs=[pl.BlockSpec(memory_space=pltpu.VMEM)],
        out_specs=pl.BlockSpec(memory_space=pltpu.VMEM),
        scratch_shapes=[
            pltpu.VMEM(pieces.shape, f32),
            pltpu.SemaphoreType.DMA((count,)),
            pltpu.SemaphoreType.DMA((count,)),
        ],
        compiler_params=pltpu.CompilerParams(
            collective_id=0, has_side_effects=True, vmem_limit_bytes=32 * 2**20
        ),
        cost_estimate=pl.CostEstimate(
            flops=pieces.size, bytes_accessed=8 * pieces.size, transcendentals=0
        ),
    )(pieces)


def on_device(
    queries,
    key_vectors,
    value_vectors,
    frozen_grad,
    output_grad,
    document_ids,
    document_tenant,
    tenant_owner,
    phm_rule,
    phm_left,
    phm_right,
):
    rows = queries.shape[0]
    reach = (WINDOW + rows - 2) // rows
    seq_count = lax.axis_size("seq")
    head_count = lax.axis_size("head")
    seq_index = lax.axis_index("seq")
    head_index = lax.axis_index("head")
    tenants = tenant_owner.shape[0]
    block_count = PHM_N // head_count
    block_start = head_index * block_count
    factor_columns = tenants * PHM_N
    sub_left, sub_right = phm_left.shape[2], phm_right.shape[2]

    rule = phm_rule.transpose(2, 3, 0, 1).reshape(PHM_N, PHM_N, factor_columns)
    left = phm_left.reshape(factor_columns, sub_left)
    right = phm_right.reshape(factor_columns, sub_right)

    lead = jnp.full((reach * rows,), -1, jnp.int32)
    key_docs = lax.dynamic_slice_in_dim(
        jnp.concatenate([lead, document_ids]), seq_index * rows, (reach + 1) * rows
    )
    query_docs = key_docs[reach * rows :]
    documents = jnp.arange(document_tenant.shape[0], dtype=jnp.int32)
    token_tenant = jnp.sum(
        jnp.where(query_docs[:, None] == documents[None, :], document_tenant[None, :], 0), axis=1
    )
    qinfo = jnp.stack([query_docs, token_tenant], axis=1)

    shifted = jnp.concatenate(
        [
            jnp.pad(right, ((0, 0), (b * sub_right, (block_count - 1 - b) * sub_right)))
            for b in range(block_count)
        ],
        axis=0,
    )
    shifted_hi, shifted_lo = split_two(shifted)
    gate_params = jnp.concatenate([shifted_hi, shifted_lo], axis=0)
    left_hi, left_lo = split_two(left)
    query_grad, key_grad, value_grad, left_sum, right_both, rule_here = main_call(
        seq_count, head_count, reach,
        (queries, key_vectors, value_vectors, frozen_grad, output_grad, gate_params, qinfo,
         key_docs[None, :], rule, left_hi, left_lo),
    )
    right_sum = sum(
        right_both[b, :, b * sub_right : (b + 1) * sub_right] for b in range(block_count)
    )
    rule_sum = lax.dynamic_update_slice_in_dim(
        jnp.zeros((PHM_N, PHM_N, factor_columns), f32), rule_here, block_start, 0
    ).transpose(2, 0, 1)

    count = seq_count * head_count
    grad_scale = rows ** (-0.5)
    flat = jnp.concatenate(
        [
            right_sum.reshape(count, -1),
            left_sum.reshape(count, -1),
            rule_sum.reshape(count, -1),
        ],
        axis=1,
    )
    size = flat.shape[1]
    padded = -(-size // 1024) * 1024
    flat = jnp.pad(flat * grad_scale, ((0, 0), (0, padded - size)))
    slots = jnp.arange(tenants, dtype=jnp.int32)
    owner_hot = (tenant_owner[None, :] == slots[:, None])[:, :, None, None, None]
    rows_by_tenant = flat.reshape(1, tenants, head_count, padded // 128, 128)
    pieces = jnp.sum(jnp.where(owner_hot, rows_by_tenant, 0.0), axis=1)
    summed = exchange_sum(pieces.reshape(count, padded // 128, 128), seq_count, head_count)
    summed = summed.reshape(-1)
    factors = PHM_N // head_count
    right_end = factors * sub_right
    left_end = right_end + factors * sub_left
    right_grad = summed[:right_end].reshape(1, factors, sub_right)
    left_grad = summed[right_end:left_end].reshape(1, factors, sub_left)
    rule_grad = summed[left_end:size].reshape(1, factors, PHM_N, PHM_N)

    return (query_grad, key_grad, value_grad, rule_grad, left_grad, right_grad)


def solution(mesh):
    rows = P(("groups", "seq"), "head")
    in_specs = (
        rows, rows, rows, rows, rows,
        P("groups"),
        P("groups"),
        P(),
        P("groups", None, None, None),
        P("groups", None, None),
        P("groups", None, None),
    )
    out_specs = (
        rows, rows, rows,
        P(("groups", "seq"), "head", None, None),
        P(("groups", "seq"), "head", None),
        P(("groups", "seq"), "head", None),
    )
    return jax.shard_map(
        on_device, mesh=mesh, in_specs=in_specs, out_specs=out_specs, check_vma=False
    )
```
